32 devices in a mesh: fsdp: 4 (over y, x), ctx: 8 (over z, core).
Axes of the slice: x: 2, y: 2, z: 4, core: 2. Of those that a mesh axis runs over, the one named last changes fastest.
Arguments:
- x_in: bfloat16 [8, 2048, 960], P('fsdp', 'ctx'), may hold values from -6 to 6
- positions: int32 [8, 2048], P('fsdp'), may hold values from 0 to 2047, as said below
- norm_one: bfloat16 [960], P('fsdp'), may hold values from 0.099609375 to 1.8984375
- w_query: bfloat16 [960, 960], P('fsdp'), may hold values from -0.1875 to 0.1875
- w_key: bfloat16 [960, 320], P('fsdp'), may hold values from -0.1875 to 0.1875
- w_value: bfloat16 [960, 320], P('fsdp'), may hold values from -0.1875 to 0.1875
- w_output: bfloat16 [960, 960], P('fsdp'), may hold values from -6 to 6
- norm_two: bfloat16 [960], P('fsdp'), may hold values from 0.099609375 to 1.8984375
- w_gate: bfloat16 [960, 2560], P('fsdp'), may hold values from -0.1875 to 0.1875
- w_up: bfloat16 [960, 2560], P('fsdp'), may hold values from -0.1875 to 0.1875
- w_down: bfloat16 [2560, 960], P('fsdp'), may hold values from -0.125 to 0.125
- cotangent: bfloat16 [8, 2048, 960], P('fsdp', 'ctx'), may hold values from -6 to 6
Outputs:
- out: bfloat16 [8, 2048, 960], P('fsdp', 'ctx')
- grad_in: bfloat16 [8, 2048, 960], P('fsdp', 'ctx')
- grad_norm_one: float32 [960], P('fsdp')
- grad_w_query: float32 [960, 960], P('fsdp')
- grad_w_key: float32 [960, 320], P('fsdp')
- grad_w_value: float32 [960, 320], P('fsdp')
- grad_w_output: float32 [960, 960], P('fsdp')
- grad_norm_two: float32 [960], P('fsdp')
- grad_w_gate: float32 [960, 2560], P('fsdp')
- grad_w_up: float32 [960, 2560], P('fsdp')
- grad_w_down: float32 [2560, 960], P('fsdp')
The draws below stay inside these ranges and needn't reach their ends.
Inputs may be any that keep to these rules, and one draw needn't show every extreme that they name: In each sequence the rows form aligned blocks of 256; the rows of a block hold 256 consecutive positions in order, and the blocks' first positions are the multiples of 256 below 2048 in some order, each once.
All inputs are finite; a program needn't handle non-finite values.
Results may differ from the reference program's by a relative error of at most 0.02.
Values may be sent and summed in bfloat16 or wider, within the bound.
A program may use at most 192 MiB of HBM per device.

```python
import math
import jax
import jax.numpy as jnp
from jax import lax

D = 960
HEADS = 15
KV_HEADS = 5
HEAD = 64
FF = 2560
SEQ_LEN = 2048
BLK = 256
SEQS = 8


def draw_positions(key, part):
    key = jax.random.fold_in(key, 11)
    count = SEQ_LEN // BLK
    seq_keys = jax.random.split(key, SEQS)
    orders = jax.vmap(lambda seq_key: jax.random.permutation(seq_key, count))(seq_keys)
    offsets = jnp.arange(BLK, dtype=jnp.int32)
    places = orders.astype(jnp.int32)[:, :, None] * BLK + offsets[None, None, :]
    return places.reshape(SEQS, SEQ_LEN)


def block_scale(rng, shape, pieces, least, largest):
    def one(axis_at, parts):
        heights = jax.random.uniform(jax.random.fold_in(jax.random.fold_in(rng, 6), axis_at), (parts,), jnp.float32, least / len(pieces), largest / len(pieces))
        return jnp.repeat(jnp.exp(heights), shape[axis_at] // parts).reshape((-1,) + (1,) * (len(shape) - axis_at - 1))

    level = one(*pieces[0])
    for cut in pieces[1:]:
        level = level * one(*cut)
    return level


def normal_values(rng, extent, deviation, limit, cuts=(), held_as=jnp.bfloat16):
    factor_of = block_scale(rng, extent, cuts, -0.22, 0.18) if cuts else 1.0
    values = jax.random.normal(rng, extent, jnp.float32) * deviation * factor_of
    return jnp.minimum(jnp.maximum(values, -limit), limit).astype(held_as)


def setup_inputs(seed: int = 0) -> dict:
    key_list = jax.random.split(jax.random.key(seed), 13)
    return {
        "x_in": normal_values(key_list[0], (SEQS, SEQ_LEN, D), 1.0, 6.0, ((0, 4), (1, 8))),
        "positions": draw_positions(jax.random.fold_in(key_list[12], 71), 0),
        "norm_one": jnp.clip(1.0 + 0.18 * jax.random.normal(key_list[2], (D,), jnp.float32), 0.099609375, 1.8984375).astype(jnp.bfloat16),
        "w_query": normal_values(key_list[3], (D, HEADS * HEAD), D ** -0.5, 0.1875, ((0, 4),)),
        "w_key": normal_values(key_list[4], (D, KV_HEADS * HEAD), D ** -0.5, 0.1875, ((0, 4),)),
        "w_value": normal_values(key_list[5], (D, KV_HEADS * HEAD), D ** -0.5, 0.1875, ((0, 4),)),
        "w_output": normal_values(key_list[6], (HEADS * HEAD, D), (max(1, HEADS * HEAD * 4 // SEQ_LEN)) ** -0.5, 6.0, ((0, 4),)),
        "norm_two": jnp.clip(1.0 + 0.18 * jax.random.normal(key_list[7], (D,), jnp.float32), 0.099609375, 1.8984375).astype(jnp.bfloat16),
        "w_gate": normal_values(key_list[8], (D, FF), D ** -0.5, 0.1875, ((0, 4),)),
        "w_up": normal_values(key_list[9], (D, FF), D ** -0.5, 0.1875, ((0, 4),)),
        "w_down": normal_values(key_list[10], (FF, D), FF ** -0.5, 0.125, ((0, 4),)),
        "cotangent": normal_values(key_list[11], (SEQS, SEQ_LEN, D), 1.0, 6.0, ((0, 4), (1, 8))),
    }


@jax.custom_vjp
def low(v):
    return lax.optimization_barrier(v.astype(jnp.bfloat16)).astype(jnp.float32)

@jax.custom_vjp
def low_back(v):
    return v

def low_keep(v):
    return (low(v), None)

def low_pass(kept, grad):
    return (grad,)

def back_keep(v):
    return (v, None)

def back_low(kept, grad):
    return (low(grad),)
low.defvjp(low_keep, low_pass)
low_back.defvjp(back_keep, back_low)
epsilon = 1e-05
rope_log_base = math.log(100000.0)
masked_value = -1e+30

def matmul(left, right):
    return jnp.dot(left, right, preferred_element_type=jnp.float32, precision=lax.Precision.HIGHEST)

def normalize(values, gain):
    inverse_scale = lax.rsqrt(lax.optimization_barrier(jnp.mean(values * values, axis=1, keepdims=True)) + epsilon)
    return values * inverse_scale * gain

def angle_tables(places):
    half = HEAD // 2
    freqs = jnp.exp(-rope_log_base * (2.0 * jnp.arange(half, dtype=jnp.float32) / HEAD))
    angles = places.astype(jnp.float32)[:, None, None] * freqs[None, None, :]
    return (jnp.cos(angles), jnp.sin(angles))

def rotate(values, cosine, sine):
    half = values.shape[-1] // 2
    first = values[..., :half]
    second = values[..., half:]
    return jnp.concatenate([first * cosine - second * sine, second * cosine + first * sine], axis=-1)

def attend_block(query, query_places, keys, values, key_places):
    scale = 1.0 / math.sqrt(HEAD)
    logits = low_back(jnp.einsum('rgah,kgh->gark', query, keys, precision=lax.Precision.HIGHEST) * scale)
    allowed = key_places[None, None, None, :] <= query_places[None, None, :, None]
    peak = lax.optimization_barrier(jnp.max(jnp.where(allowed, logits, masked_value), axis=3, keepdims=True))
    total = lax.optimization_barrier(jnp.sum(jnp.exp(jnp.where(allowed, logits - peak, masked_value)), axis=3, keepdims=True))
    shift = peak + jnp.log(total)
    weights = low(jnp.exp(jnp.where(allowed, logits - shift, masked_value)))
    return jnp.einsum('gark,kgh->rgah', weights, values, precision=lax.Precision.HIGHEST)

def layer(inputs, places, gain_one, query_w, key_w, value_w, output_w, gain_two, gate_w, up_w, down_w):
    length = inputs.shape[0]
    groups = HEADS // KV_HEADS
    normed_one = low(normalize(inputs, gain_one))
    q_raw = low_back(matmul(normed_one, query_w))
    k_raw = low_back(matmul(normed_one, key_w))
    value = low(low_back(matmul(normed_one, value_w)))
    cosine, sine = angle_tables(places)
    query = low(rotate(q_raw.reshape(length, HEADS, HEAD), cosine, sine))
    key = low(rotate(k_raw.reshape(length, KV_HEADS, HEAD), cosine, sine))
    value_heads = value.reshape(length, KV_HEADS, HEAD)
    block = min(512, length)
    count = length // block
    query_blocks = query.reshape(count, block, KV_HEADS, groups, HEAD)
    place_blocks = places.reshape(count, block)
    checked = jax.checkpoint(attend_block)

    def one_block(element):
        return checked(element[0], element[1], key, value_heads, places)
    attended = lax.map(one_block, (query_blocks, place_blocks)).reshape(length, HEADS * HEAD)
    attended = low(low_back(attended))
    hidden = inputs + low_back(matmul(attended, output_w))
    normed_two = low(normalize(hidden, gain_two))
    gate = low_back(matmul(normed_two, gate_w))
    upper = low_back(matmul(normed_two, up_w))
    activated = low(jax.nn.silu(gate) * upper)
    return hidden + low_back(matmul(activated, down_w))

def reference(x_in, positions, norm_one, w_query, w_key, w_value, w_output, norm_two, w_gate, w_up, w_down, cotangent):
    params = (norm_one.astype(jnp.float32), w_query.astype(jnp.float32), w_key.astype(jnp.float32), w_value.astype(jnp.float32), w_output.astype(jnp.float32), norm_two.astype(jnp.float32), w_gate.astype(jnp.float32), w_up.astype(jnp.float32), w_down.astype(jnp.float32))

    def one_sequence(carry, element):
        rows_in, places, upstream = element

        def forward(inputs, gain_one, query_w, key_w, value_w, output_w, gain_two, gate_w, up_w, down_w):
            return layer(inputs, places, gain_one, query_w, key_w, value_w, output_w, gain_two, gate_w, up_w, down_w)
        result, pullback = jax.vjp(forward, rows_in.astype(jnp.float32), *params)
        grads = pullback(upstream.astype(jnp.float32))
        summed = tuple(jax.tree.map(lambda earlier, later: earlier + later, carry, tuple(grads[1:])))
        return (summed, (result.astype(jnp.bfloat16), grads[0].astype(jnp.bfloat16)))
    start = tuple(jax.tree.map(lambda param: jnp.zeros(param.shape, jnp.float32), params))
    sums, outputs = lax.scan(one_sequence, start, (x_in, positions, cotangent))
    return (outputs[0], outputs[1], sums[0], sums[1], sums[2], sums[3], sums[4], sums[5], sums[6], sums[7], sums[8])
```

```python
import math

import jax
import jax.numpy as jnp
from jax import lax
from jax.experimental import pallas as pl
from jax.experimental.pallas import tpu as pltpu
from jax.sharding import PartitionSpec as P

HEADS = 15
KV_HEADS = 5
HEAD = 64


epsilon = 1e-05
rope_log_base = math.log(100000.0)
masked_value = -1e30


def matmul(left, right):
    return jnp.dot(left, right, preferred_element_type=jnp.float32)


def left_transposed(left, right):
    return lax.dot_general(
        left, right, (((0,), (0,)), ((), ())), preferred_element_type=jnp.float32
    )


def right_transposed(left, right):
    return lax.dot_general(
        left, right, (((1,), (1,)), ((), ())), preferred_element_type=jnp.float32
    )


def angle_tables(places):
    half = HEAD // 2
    freqs = jnp.exp(-rope_log_base * (2.0 * jnp.arange(half, dtype=jnp.float32) / HEAD))
    angles = places.astype(jnp.float32)[..., None] * freqs
    cosine, sine = jnp.cos(angles), jnp.sin(angles)
    return (
        jnp.concatenate([cosine, cosine], axis=-1),
        jnp.concatenate([-sine, sine], axis=-1),
    )


def swap_halves(values):
    half = HEAD // 2
    return jnp.concatenate([values[:, half:], values[:, :half]], axis=1)


def turn(values, cosine, sine):
    half = HEAD // 2
    heads = values.shape[1] // HEAD
    lane = lax.broadcasted_iota(jnp.int32, values.shape, 1)
    swapped = jnp.where(
        lax.rem(lane, HEAD) < half, jnp.roll(values, -half, axis=1), jnp.roll(values, half, axis=1)
    )
    return values * jnp.tile(cosine, (1, heads)) + swapped * jnp.tile(sine, (1, heads))


def norm_forward(values, gain):
    inverse_scale = lax.rsqrt(jnp.mean(values * values, axis=1, keepdims=True) + epsilon)
    return (values * inverse_scale * gain, inverse_scale)


def norm_backward(values, inverse_scale, gain, upstream):
    scaled = gain * upstream
    inner = jnp.mean(scaled * values, axis=1, keepdims=True)
    grad_values = (
        inverse_scale * scaled - values * (inverse_scale * inverse_scale * inverse_scale) * inner
    )
    grad_gain = jnp.sum(upstream * values * inverse_scale, axis=0)
    return (grad_values, grad_gain)


def contract_last(left, right):
    return lax.dot_general(
        left, right, (((1,), (1,)), ((), ())), preferred_element_type=jnp.float32
    )


def forward_kernel(
    raw_ref, key_ref, value_ref, own_ref, place_ref, cos_ref, sin_ref, query_ref, out_ref, lse_ref, bias_ref
):
    groups = HEADS // KV_HEADS
    bias_ref[...] = jnp.where(place_ref[0] <= own_ref[0], 0.0, masked_value)
    cosine, sine = cos_ref[0], sin_ref[0]
    length = key_ref.shape[1]
    for kv in range(KV_HEADS):
        kv_lanes = slice(kv * HEAD, (kv + 1) * HEAD)
        keys = key_ref[0, :, kv_lanes]
        values = value_ref[0, :, kv_lanes].astype(jnp.float32).T.astype(jnp.bfloat16)
        values = jnp.concatenate([values, jnp.ones((16, length), jnp.bfloat16)], axis=0)
        for head in range(kv * groups, (kv + 1) * groups):
            lanes = slice(head * HEAD, (head + 1) * HEAD)
            raw = raw_ref[0, :, lanes]
            query = (raw * cosine + swap_halves(raw) * sine).astype(jnp.bfloat16)
            query_ref[0, :, lanes] = query
            logits = contract_last(keys, query * 0.125) + bias_ref[...]
            peak = jnp.max(logits, axis=0, keepdims=True)
            terms = jnp.exp(logits - peak).astype(jnp.bfloat16)
            summed = matmul(values, terms)
            total = summed[HEAD : HEAD + 1]
            lse_ref[0, head : head + 1, :] = peak + jnp.log(total)
            out_ref[0, :, lanes] = (summed[:HEAD] / total).T.astype(jnp.bfloat16)


def backward_kernel(
    query_ref, up_ref, out_ref, key_ref, value_ref, own_ref, place_ref, cos_ref, sin_ref, lse_ref,
    grad_query_ref, grad_key_ref, grad_value_ref, bias_ref,
):
    groups = HEADS // KV_HEADS
    rows = query_ref.shape[1]
    length = key_ref.shape[1]
    block = min(512, length)
    one = jnp.where(place_ref[0] <= own_ref[0], 0.0, masked_value)
    bias_ref[...] = jnp.concatenate([one] * groups, axis=1)
    cosine, sine = cos_ref[0], sin_ref[0]
    for kv in range(KV_HEADS):
        kv_lanes = slice(kv * HEAD, (kv + 1) * HEAD)
        heads = range(kv * groups, (kv + 1) * groups)
        queries, ups, shifts, deltas = [], [], [], []
        for head in heads:
            lanes = slice(head * HEAD, (head + 1) * HEAD)
            up = up_ref[0, :, lanes]
            product = up.astype(jnp.float32) * out_ref[0, :, lanes].astype(jnp.float32)
            queries.append(query_ref[0, :, lanes] * 0.125)
            ups.append(up)
            shifts.append(lse_ref[0, head : head + 1, :])
            deltas.append(jnp.sum(product.T, axis=0, keepdims=True))
        query = jnp.concatenate(queries, axis=0)
        upstream = jnp.concatenate(ups, axis=0)
        shift = jnp.concatenate(shifts, axis=1)
        delta = jnp.concatenate(deltas, axis=1)
        total = jnp.zeros((HEAD, groups * rows), jnp.float32)
        for start in range(0, length, block):
            span = slice(start, start + block)
            keys = key_ref[0, span, kv_lanes]
            values = value_ref[0, span, kv_lanes]
            logits = contract_last(keys, query) + bias_ref[span, :]
            weights = jnp.exp(logits - shift)
            grad_weights = contract_last(values, upstream)
            grad_logits = (weights * (grad_weights - delta)).astype(jnp.bfloat16)
            grad_value = matmul(weights.astype(jnp.bfloat16), upstream)
            grad_key = matmul(grad_logits, query)
            grad_value_ref[0, span, kv_lanes] = grad_value.astype(jnp.bfloat16)
            grad_key_ref[0, span, kv_lanes] = grad_key.astype(jnp.bfloat16)
            total += matmul(keys.astype(jnp.float32).T.astype(jnp.bfloat16), grad_logits)
        total = total * 0.125
        for at, head in enumerate(heads):
            grad = total[:, at * rows : (at + 1) * rows].T
            grad = grad * cosine - swap_halves(grad) * sine
            grad_query_ref[0, :, head * HEAD : (head + 1) * HEAD] = grad.astype(jnp.bfloat16)


def whole_block(array):
    return pl.BlockSpec((1,) + array.shape[1:], lambda at: (at, 0, 0))


def attend_forward(raw, keys, values, own_places, places, cosine, sine):
    seqs, rows, width = raw.shape
    length = keys.shape[1]
    operands = (raw, keys, values, own_places[:, None, :], places[:, :, None], cosine, sine)
    outs = (
        jax.ShapeDtypeStruct(raw.shape, jnp.bfloat16),
        jax.ShapeDtypeStruct(raw.shape, jnp.bfloat16),
        jax.ShapeDtypeStruct((seqs, HEADS, rows), jnp.float32),
    )
    pairs = seqs * rows * length * HEADS
    return pl.pallas_call(
        forward_kernel,
        grid=(seqs,),
        in_specs=[whole_block(array) for array in operands],
        out_specs=[whole_block(array) for array in outs],
        out_shape=outs,
        scratch_shapes=[pltpu.VMEM((length, rows), jnp.float32)],
        compiler_params=pltpu.CompilerParams(vmem_limit_bytes=48 * 1024 * 1024),
        cost_estimate=pl.CostEstimate(
            flops=8 * pairs * HEAD, bytes_accessed=4 * raw.size * 3, transcendentals=pairs
        ),
    )(*operands)


def attend_backward(query, upstream, output, keys, values, own_places, places, cosine, sine, lse):
    seqs, rows, width = query.shape
    length = keys.shape[1]
    operands = (
        query, upstream, output, keys, values,
        own_places[:, None, :], places[:, :, None], cosine, sine, lse,
    )
    outs = (
        jax.ShapeDtypeStruct(query.shape, jnp.bfloat16),
        jax.ShapeDtypeStruct(keys.shape, jnp.bfloat16),
        jax.ShapeDtypeStruct(values.shape, jnp.bfloat16),
    )
    pairs = seqs * rows * length * HEADS
    return pl.pallas_call(
        backward_kernel,
        grid=(seqs,),
        in_specs=[whole_block(array) for array in operands],
        out_specs=[whole_block(array) for array in outs],
        out_shape=outs,
        scratch_shapes=[pltpu.VMEM((length, rows * (HEADS // KV_HEADS)), jnp.float32)],
        compiler_params=pltpu.CompilerParams(vmem_limit_bytes=56 * 1024 * 1024),
        cost_estimate=pl.CostEstimate(
            flops=20 * pairs * HEAD, bytes_accessed=4 * query.size * 3, transcendentals=pairs
        ),
    )(*operands)


def half_of(array, which):
    size = array.shape[1] // 2
    return lax.dynamic_slice_in_dim(array, which * size, size, 1)


def core_swap(array):
    count = lax.axis_size("ctx")
    return lax.ppermute(array, "ctx", [(at, at ^ 1) for at in range(count)])


def join_halves(mine, other, which):
    first = which == 0
    return jnp.concatenate(
        [jnp.where(first, mine, other), jnp.where(first, other, mine)], axis=1
    )


def gather_weight(shard, which):
    mine = lax.all_gather(half_of(shard, which), "fsdp", axis=0, tiled=True)
    return join_halves(mine, core_swap(mine), which)


def start_share(left, right, which):
    theirs = left_transposed(left, half_of(right, 1 - which)).astype(jnp.bfloat16)
    got = core_swap(theirs).astype(jnp.float32)
    mine = left_transposed(left, half_of(right, which)) + got
    return mine.astype(jnp.bfloat16)


def scatter_share(mine):
    return lax.psum_scatter(mine, "fsdp", scatter_dimension=0, tiled=True)


def sum_share(part, which):
    count = lax.axis_size("ctx")
    groups = [list(range(0, count, 2)), list(range(1, count, 2))]
    mine = lax.psum(part, "ctx", axis_index_groups=groups)
    return join_halves(mine, core_swap(mine), which).astype(jnp.float32)


def on_device(
    x_in,
    positions,
    norm_one,
    w_query,
    w_key,
    w_value,
    w_output,
    norm_two,
    w_gate,
    w_up,
    w_down,
    cotangent,
):
    seqs, rows, width = x_in.shape
    total_rows = seqs * rows
    kv_width = KV_HEADS * HEAD
    which = lax.rem(lax.axis_index("ctx"), 2)
    at_key, at_value = width, width + kv_width
    at_gain = width + 2 * kv_width
    padded = -(-(at_gain + 2) // 256) * 256
    packed = jnp.concatenate(
        [
            w_query,
            w_key,
            w_value,
            norm_one[:, None],
            norm_two[:, None],
            jnp.zeros((w_query.shape[0], padded - at_gain - 2), jnp.bfloat16),
        ],
        axis=1,
    )
    packed = gather_weight(packed, which)
    query_w, key_w = packed[:, :at_key], packed[:, at_key:at_value]
    value_w = packed[:, at_value:at_gain]
    gain_one, gain_two = packed[:, at_gain], packed[:, at_gain + 1]
    output_w = gather_weight(w_output, which)
    gate_w = gather_weight(w_gate, which)
    up_w = gather_weight(w_up, which)
    down_w = gather_weight(w_down, which)
    own_places = lax.dynamic_slice_in_dim(positions, lax.axis_index("ctx") * rows, rows, 1)
    table_cos, table_sin = angle_tables(own_places)
    cosine, sine = table_cos.reshape(total_rows, HEAD), table_sin.reshape(total_rows, HEAD)
    inputs = x_in.reshape(total_rows, width).astype(jnp.float32)
    first_gain = gain_one.astype(jnp.float32)
    normed, first_scale = norm_forward(inputs, first_gain)
    normed_one = normed.astype(jnp.bfloat16)
    raw_query = matmul(normed_one, query_w).reshape(seqs, rows, width)
    own_keys = turn(matmul(normed_one, key_w), cosine, sine)
    own_keys = own_keys.astype(jnp.bfloat16).reshape(seqs, rows, kv_width)
    own_values = matmul(normed_one, value_w).astype(jnp.bfloat16).reshape(seqs, rows, kv_width)
    all_keys, all_values = (
        lax.all_gather(own_keys, "ctx", axis=1, tiled=True),
        lax.all_gather(own_values, "ctx", axis=1, tiled=True),
    )
    query, attended, lse = attend_forward(
        raw_query, all_keys, all_values, own_places, positions, table_cos, table_sin
    )
    attended_low = attended.reshape(total_rows, HEADS * HEAD)
    hidden = inputs + matmul(attended_low, output_w)
    second_gain = gain_two.astype(jnp.float32)
    normed, second_scale = norm_forward(hidden, second_gain)
    normed_two = normed.astype(jnp.bfloat16)
    gate = matmul(normed_two, gate_w)
    upper = matmul(normed_two, up_w)
    sigmoid = jax.nn.sigmoid(gate)
    activated = (gate * sigmoid * upper).astype(jnp.bfloat16)
    output = hidden + matmul(activated, down_w)
    upstream = cotangent.reshape(total_rows, width)
    grad_act = right_transposed(upstream, down_w)
    grad_gate = (grad_act * upper * sigmoid * (1.0 + gate * (1.0 - sigmoid))).astype(jnp.bfloat16)
    grad_upper = (grad_act * gate * sigmoid).astype(jnp.bfloat16)
    grad_normed_two = right_transposed(grad_gate, gate_w) + right_transposed(grad_upper, up_w)
    grad_hidden, grad_gain_two = norm_backward(hidden, second_scale, second_gain, grad_normed_two)
    grad_hidden = grad_hidden + upstream.astype(jnp.float32)
    grad_branch = grad_hidden.astype(jnp.bfloat16)
    grad_attended = right_transposed(grad_branch, output_w).astype(jnp.bfloat16)
    early = tuple(
        start_share(left, right, which)
        for left, right in (
            (activated, upstream),
            (normed_two, grad_gate),
            (normed_two, grad_upper),
            (attended_low, grad_branch),
        )
    )
    grad_attended, early = lax.optimization_barrier((grad_attended, early))
    first_part = scatter_share(early[0])
    grad_query, grad_keys, grad_values = attend_backward(
        query, grad_attended.reshape(seqs, rows, width), attended, all_keys, all_values,
        own_places, positions, table_cos, table_sin, lse,
    )
    grad_keys, grad_values, first_part = lax.optimization_barrier(
        (grad_keys, grad_values, first_part)
    )
    own_grad_keys, own_grad_values = (
        lax.psum_scatter(
            grad_keys,
            "ctx",
            scatter_dimension=1,
            tiled=True,
        ).astype(jnp.float32),
        lax.psum_scatter(
            grad_values,
            "ctx",
            scatter_dimension=1,
            tiled=True,
        ).astype(jnp.float32),
    )
    grad_query_low = grad_query.reshape(total_rows, HEADS * HEAD)
    grad_key_low = turn(own_grad_keys.reshape(total_rows, kv_width), cosine, -sine)
    grad_key_low = grad_key_low.astype(jnp.bfloat16)
    grad_value_low = own_grad_values.reshape(total_rows, kv_width).astype(jnp.bfloat16)
    grad_normed_one = (
        right_transposed(grad_query_low, query_w)
        + right_transposed(grad_key_low, key_w)
        + right_transposed(grad_value_low, value_w)
    )
    grad_inputs, grad_gain_one = norm_backward(inputs, first_scale, first_gain, grad_normed_one)
    grad_inputs = grad_inputs + grad_hidden
    result_out = output.astype(jnp.bfloat16).reshape(seqs, rows, width)
    result_grad = grad_inputs.astype(jnp.bfloat16).reshape(seqs, rows, width)
    own_grad_keys, own_grad_values, rest = lax.optimization_barrier(
        (own_grad_keys, own_grad_values, early[1:])
    )
    parts = (first_part,) + tuple(scatter_share(share) for share in rest)
    rights = jnp.concatenate(
        [
            grad_query_low,
            grad_key_low,
            grad_value_low,
            jnp.zeros((total_rows, padded - at_gain), jnp.bfloat16),
        ],
        axis=1,
    )
    late = start_share(normed_one, rights, which)
    late_part = scatter_share(late)
    sums = tuple(sum_share(part, which) for part in parts)
    late_sum = sum_share(late_part, which)
    gains = lax.psum(jnp.stack([grad_gain_one, grad_gain_two]), ("fsdp", "ctx"))
    own_rows = norm_one.shape[0]
    gains = lax.dynamic_slice_in_dim(gains, lax.axis_index("fsdp") * own_rows, own_rows, 1)
    return (
        result_out,
        result_grad,
        gains[0],
        late_sum[:, :at_key],
        late_sum[:, at_key:at_value],
        late_sum[:, at_value:at_gain],
        sums[3],
        gains[1],
        sums[1],
        sums[2],
        sums[0],
    )


def solution(mesh):
    in_specs = (
        P("fsdp", "ctx", None),
        P("fsdp", None),
        P("fsdp"),
        P("fsdp", None),
        P("fsdp", None),
        P("fsdp", None),
        P("fsdp", None),
        P("fsdp"),
        P("fsdp", None),
        P("fsdp", None),
        P("fsdp", None),
        P("fsdp", "ctx", None),
    )
    out_specs = (
        P("fsdp", "ctx", None),
        P("fsdp", "ctx", None),
        P("fsdp"),
        P("fsdp", None),
        P("fsdp", None),
        P("fsdp", None),
        P("fsdp", None),
        P("fsdp"),
        P("fsdp", None),
        P("fsdp", None),
        P("fsdp", None),
    )
    return jax.shard_map(
        on_device, mesh=mesh, in_specs=in_specs, out_specs=out_specs, check_vma=False
    )
```
